128 devices in a mesh: chan: 8 (over x, y_lo), panel: 16 (over z, y_hi, core).
Axes of the slice: x: 4, y: 4 (y_hi: 2, y_lo: 2; y = y_hi * 2 + y_lo), z: 4, core: 2. Of those that a mesh axis runs over, the one named last changes fastest.
Arguments:
- voltages: bfloat16 [2048, 536576], P(('chan', 'panel')), may hold values from -6 to 6
- prototype: float32 [4, 4096], replicated, may hold values from -0.046875 to 0.046875
- complex_gains: float32 [2048, 96], P(('chan', 'panel')), may hold values from -4 to 4
- flagged: int32 [1024], P(('chan', 'panel')), may hold values 0 or 1
- station_order: int32 [1024], replicated, may hold values from 0 to 1023, each once
Outputs:
- visibilities: bfloat16 [2, 48, 2048, 2048], P(None, 'chan', 'panel')
The draws below stay inside these ranges and needn't reach their ends.
Inputs may be any that keep to these rules, and one draw needn't show every extreme that they name: `station_order`: each station appears once.
All inputs are finite; a program needn't handle non-finite values. No bound on the sum of `flagged` on one device may be relied on, other than what follows from the above.
Results may differ from the reference program's by a relative error of at most 0.0073.
Values may be sent and summed in bfloat16 or wider, within the bound.
A program may use at most 128 MiB of HBM per device.

```python
import math
import jax
import jax.numpy as jnp
from jax import lax

NFFT = 4096
TAPS = 4
STA_DEV = 8
FRAMES = 128
STATIONS = 1024
INPUTS = 2048
NCHAN = 48


def touch_ends(entries, key, low, largest):
    extent = entries.shape
    index_at = [jax.random.randint(jax.random.fold_in(key, axis), (), 0, extent[axis]) for axis in range(len(extent))]
    entries = entries.at[tuple(index_at)].set(low)
    longest = extent.index(max(extent))
    index_at[longest] = (index_at[longest] + 1) % extent[longest]
    return entries.at[tuple(index_at)].set(largest)


def level_of(own_key, extent, cuts, least, top_value):
    def one(axis_at, blocks):
        heights = jax.random.uniform(jax.random.fold_in(jax.random.fold_in(own_key, 6), axis_at), (blocks,), jnp.float32, least / len(cuts), top_value / len(cuts))
        return jnp.repeat(jnp.exp(heights), extent[axis_at] // blocks).reshape((-1,) + (1,) * (len(extent) - axis_at - 1))

    level = one(*cuts[0])
    for cut in cuts[1:]:
        level = level * one(*cut)
    return level


def scatter_about(own_key, dims, spread, reach, cuts=(), kind=jnp.bfloat16):
    entries = jax.random.normal(own_key, dims, jnp.float32) * spread
    if len(cuts) > 0:
        entries = level_of(own_key, dims, cuts, -0.22, 0.18) * entries
    return jnp.clip(entries, min=-reach, max=reach).astype(kind)


def setup_inputs(seed: int = 0) -> dict:
    streams_of = jax.random.split(jax.random.key(seed), 6)
    voltages = scatter_about(streams_of[0], (INPUTS, (FRAMES + TAPS - 1) * NFFT), 1.0, 6.0, ((0, 128),))
    prototype = scatter_about(streams_of[1], (TAPS, NFFT), (TAPS * NFFT) ** -0.5, 0.046875, (), jnp.float32)
    complex_gains = scatter_about(streams_of[2], (INPUTS, 2 * NCHAN), 0.7, 4.0, ((0, 128),), jnp.float32)
    flagged = touch_ends((jax.random.randint(streams_of[3], (STATIONS,), 0, 8) < 1).astype(jnp.int32), jax.random.fold_in(streams_of[3], 1), 0, 1)
    station_order = jax.random.permutation(streams_of[4], STATIONS).astype(jnp.int32)
    return dict(voltages=voltages, prototype=prototype, complex_gains=complex_gains, flagged=flagged, station_order=station_order)


def make_table(length, channels):
    sample = jnp.arange(length, dtype=jnp.int32)[:, None]
    column = length // 4 + jnp.arange(channels, dtype=jnp.int32)[None, :]
    phases = ((sample * column) % length).astype(jnp.float32) * (2.0 * math.pi / length)
    stacked = jnp.stack([jnp.cos(phases), -jnp.sin(phases)], axis=2)
    return stacked.reshape(length, 2 * channels).astype(jnp.bfloat16)


def windowed(shaped_volt, prototype, count):
    accumulated = jnp.zeros((shaped_volt.shape[0], count, shaped_volt.shape[2]), jnp.float32)
    for tap_index in range(prototype.shape[0]):
        accumulated = accumulated + prototype[tap_index][None, None, :] * shaped_volt[:, tap_index:tap_index + count, :].astype(jnp.float32)
    return accumulated.astype(jnp.bfloat16)


def spectra_of(shaped_volt, prototype, dft_table, complex_gains, keeping, count):
    frames_win = windowed(shaped_volt, prototype, count)
    raw_spectra = jnp.einsum("nk,ifn->kif", dft_table.astype(jnp.float32), frames_win.astype(jnp.float32))
    channels = dft_table.shape[1] // 2
    local_inputs = shaped_volt.shape[0]
    shaped = raw_spectra.reshape(channels, 2, local_inputs, count)
    gain_parts = complex_gains.T.reshape(channels, 2, local_inputs)[:, :, :, None]
    real_part = gain_parts[:, 0] * shaped[:, 0] - gain_parts[:, 1] * shaped[:, 1]
    imag_part = gain_parts[:, 0] * shaped[:, 1] + gain_parts[:, 1] * shaped[:, 0]
    stacked = jnp.stack([real_part, imag_part], axis=1) * keeping[None, None, :, None]
    return stacked.astype(jnp.bfloat16)


def reference(voltages, prototype, complex_gains, flagged, station_order):
    group_size = 2 * STA_DEV
    groups = INPUTS // group_size
    shaped_volt = voltages.reshape(groups, group_size, FRAMES + TAPS - 1, NFFT)
    gains_grouped = complex_gains.reshape(groups, group_size, 2 * NCHAN)
    keeping = jnp.repeat(1.0 - flagged.astype(jnp.float32), 2).reshape(groups, group_size)
    dft_table = make_table(NFFT, NCHAN)

    def one_group(pieces):
        return spectra_of(pieces[0], prototype, dft_table, pieces[1], pieces[2], FRAMES)

    spectra = lax.map(one_group, (shaped_volt, gains_grouped, keeping))
    spectra = spectra.transpose(1, 2, 0, 3, 4).reshape(NCHAN, 2, INPUTS, FRAMES)
    position = jnp.arange(INPUTS, dtype=jnp.int32)
    source = (2 * station_order[position // 2] + position % 2).astype(jnp.int32)
    ordered = jnp.take(spectra, source, axis=2)

    def one_channel(block_pair):
        left = jnp.concatenate([block_pair[0], block_pair[1]], axis=1)
        lower = jnp.concatenate([-block_pair[1], block_pair[0]], axis=1)
        right = jnp.concatenate([left, lower], axis=0)
        product = jnp.dot(left, right.T, preferred_element_type=jnp.float32) * (1.0 / FRAMES)
        return jnp.stack([product[:, :INPUTS], product[:, INPUTS:]], axis=0).astype(jnp.bfloat16)

    result = lax.map(one_channel, ordered)
    return result.transpose(1, 0, 2, 3)
```

```python
import functools
import math

import jax
import jax.numpy as jnp
import numpy as np
from jax import lax
from jax.experimental import pallas as pl
from jax.experimental.pallas import tpu as pltpu
from jax.sharding import PartitionSpec as P

MESH = pl.DeviceIdType.MESH
F32, BF16 = jnp.float32, jnp.bfloat16
NT = (((1,), (1,)), ((), ()))

NFFT, TAPS, FRAMES, NCHAN = 4096, 4, 128, 48
INPUTS, STATIONS = 2048, 1024
LOCAL = 16
GROUPS, PER = 8, 6
FALL = FRAMES + TAPS - 1
PIECE = LOCAL * 2 * PER
BLOCK = GROUPS * PIECE
PANELS = 16
CHUNK_F = 33
STARTS = (0, 33, 66, 98)


def table_rows():
    n = np.arange(NFFT)[None, :]
    j = np.arange(NCHAN)[:, None]
    m = (n * (NFFT // 4 + j)) % NFFT
    phase = m.astype(np.float32) * np.float32(2.0 * math.pi / NFFT)
    both = np.stack([np.cos(phase), -np.sin(phase)], axis=1)
    both = both.reshape(GROUPS, PER, 2, NFFT).transpose(0, 2, 1, 3)
    both = np.pad(both, ((0, 0), (0, 0), (0, 8 - PER), (0, 0)))
    return both.reshape(128, NFFT).astype(jnp.bfloat16)


def channelize_kernel(volt, proto, table, gre, gim, out, buf, w, y, s, sems):
    def load(q):
        cols = pl.ds((STARTS[q] if q < 3 else 99) * NFFT, (33 if q < 3 else 32) * NFFT)
        return pltpu.make_async_copy(volt.at[:, cols], buf.at[:, cols], sems.at[q])

    for q in range(4):
        load(q).start()

    tab = 512

    def weights(i, _):
        cols = pl.ds(pl.multiple_of(i * tab, tab), tab)
        t = table[:, cols].astype(F32)
        for tap in range(TAPS):
            w[pl.ds(tap * 128, 128), cols] = (t * proto[tap : tap + 1, cols]).astype(BF16)
        return 0

    lax.fori_loop(0, NFFT // tab, weights, 0)

    kw = 1024
    for q in range(4):
        load(q).wait()
        first = STARTS[q]
        rows = pl.ds(first * LOCAL, CHUNK_F * LOCAL)

        def step(i, _):
            k = pl.multiple_of(i * kw, kw)
            x = jnp.concatenate([buf[:, pl.ds(k + (first + f) * NFFT, kw)] for f in range(CHUNK_F)], axis=0)
            for h in range(2):
                prod = lax.dot_general(x, w[pl.ds(h * 256, 256), pl.ds(k, kw)], NT, preferred_element_type=F32)
                for u in range(2):
                    part = prod[:, u * 128 : u * 128 + 128]
                    t = 2 * h + u

                    @pl.when(i == 0)
                    def _():
                        y[t, rows, :] = part

                    @pl.when(i > 0)
                    def _():
                        y[t, rows, :] += part
            return 0

        lax.fori_loop(0, NFFT // kw, step, 0)

    for i in range(LOCAL):
        raw = y[0, pl.ds(i, FRAMES, stride=LOCAL), :]
        for t in range(1, TAPS):
            raw = raw + y[t, pl.ds(t * LOCAL + i, FRAMES, stride=LOCAL), :]
        turned = raw.T
        for g in range(GROUPS):
            re, im = turned[g * 16 : g * 16 + 8], turned[g * 16 + 8 : g * 16 + 16]
            a, b = gre[g * 8 : g * 8 + 8, i : i + 1], gim[g * 8 : g * 8 + 8, i : i + 1]
            at = g * PIECE + i * 2 * PER
            s[at : at + PER, :] = (a * re - b * im)[:PER]
            s[at + PER : at + 2 * PER, :] = (a * im + b * re)[:PER]
    out[...] = s[...].astype(BF16)


def channelize(volt, proto, gre, gim):
    vm = pl.BlockSpec(memory_space=pltpu.VMEM)
    return pl.pallas_call(
        channelize_kernel,
        out_shape=jax.ShapeDtypeStruct((BLOCK, 128), BF16),
        in_specs=[pl.BlockSpec(memory_space=pl.ANY), vm, vm, vm, vm],
        out_specs=vm,
        scratch_shapes=[
            pltpu.VMEM((LOCAL, FALL * NFFT), BF16),
            pltpu.VMEM((TAPS * 128, NFFT), BF16),
            pltpu.VMEM((TAPS, FALL * LOCAL, 128), F32),
            pltpu.VMEM((BLOCK, 128), F32),
            pltpu.SemaphoreType.DMA((4,)),
        ],
        compiler_params=pltpu.CompilerParams(vmem_limit_bytes=56 * 2**20),
        cost_estimate=pl.CostEstimate(flops=2 * 2096 * 4096 * 512, bytes_accessed=20 * 2**20, transcendentals=0),
        name="channelize",
    )(volt, proto, jnp.asarray(table_rows()), gre, gim)


CHUNK = BLOCK // 4
HALF = CHUNK // 2
ORDER = (0, 1, 3, 2)
Z_FIRST = (0, 3)


def exchange_kernel(src, out, ss, rs, own_sem):
    c, p = lax.axis_index("chan"), lax.axis_index("panel")
    x, yl = c // 2, c % 2
    z, h, k = p // 4, (p // 2) % 2, p % 2

    def panel(dz, dh, dk=0):
        return ((z + dz) % 4) * 4 + ((h + dh) % 2) * 2 + (k + dk) % 2

    def at_panel(pan):
        return {"chan": c, "panel": pan}

    up, down, over, sib = (at_panel(a) for a in (panel(1, 0), panel(3, 0), panel(0, 1), panel(0, 0, 1)))

    def chan_target(r):
        return ((x + 4 - r // 2) % 4) * 2 + (yl + r % 2) % 2

    barrier = pltpu.get_barrier_semaphore()
    greet = [{"chan": chan_target(r), "panel": p} for r in range(1, 8)] + [up, down, over, sib]
    for d in greet:
        pl.semaphore_signal(barrier, inc=1, device_id=d, device_id_type=MESH)
    pl.semaphore_wait(barrier, len(greet))

    ids, sends = {}, []

    def number(name):
        return ids.setdefault(name, len(ids))

    def region(block, row, rows):
        return out.at[pl.ds(pl.multiple_of(block * BLOCK + row, 16), rows)]

    def send(name, block, row, rows, device, source=None):
        n = number(name)
        there = region(block, row, rows)
        copy = pltpu.make_async_remote_copy(
            there if source is None else source, there, ss.at[n], rs.at[n], device_id=device, device_id_type=MESH
        )
        copy.start()
        sends.append(copy)

    def arrived(name, block, row, rows):
        n = number(name)
        here = region(block, row, rows)
        pltpu.make_async_remote_copy(here, here, ss.at[n], rs.at[n], device_id=sib, device_id_type=MESH).wait_recv()

    shared = []

    def share(block_d, row, rows):
        name = ("s", block_d, row)
        send(name, panel(*block_d), row, rows, sib)
        shared.append((name, block_d, row, rows))

    mine = panel(0, 0)
    own = pltpu.make_async_copy(src.at[pl.ds(pl.multiple_of(c * PIECE, 16), PIECE)], region(mine, 0, PIECE), own_sem)
    own.start()
    for r in (1, 2, 3, 6, 7, 4, 5):
        t = chan_target(r)
        piece = src.at[pl.ds(pl.multiple_of(t * PIECE, 16), PIECE)]
        send(("a", r), mine, r * PIECE, PIECE, {"chan": t, "panel": p}, piece)

    def own_chunk(q):
        for r in (2 * q, 2 * q + 1):
            if r == 0:
                own.wait()
            else:
                arrived(("a", r), mine, r * PIECE, PIECE)
        row = q * CHUNK
        if q not in Z_FIRST:
            send(("y", 0, q), mine, row, CHUNK, over)
        send(("up", 0, q), mine, row, CHUNK, up)
        send(("down", 0, q), mine, row, CHUNK, down)
        if q in Z_FIRST:
            send(("y", 0, q), mine, row, CHUNK, over)
        share((0, 0), row, CHUNK)

    def near(dh, q):
        row = q * CHUNK
        for dz, got, way, half, name in ((3, "up", up, 0, "fup"), (1, "down", down, HALF, "fdown")):
            block = panel(dz, dh)
            arrived((got, dh, q), block, row, CHUNK)
            send((name, dh, q), block, row + half, HALF, way)
            if dh == 0 and q in Z_FIRST:
                send(("y", dz, q), block, row, CHUNK, over)
            share((dz, dh), row, CHUNK)

    def far(dh, q):
        row = q * CHUNK
        block = panel(2, dh)
        for name, half in (("fup", 0), ("fdown", HALF)):
            arrived((name, dh, q), block, row + half, HALF)
            if dh == 0 and q in Z_FIRST:
                send(("y", 2, q, half), block, row + half, HALF, over)
            share((2, dh), row + half, HALF)

    def partner(q):
        row, block = q * CHUNK, panel(0, 1)
        arrived(("y", 0, q), block, row, CHUNK)
        send(("up", 1, q), block, row, CHUNK, up)
        send(("down", 1, q), block, row, CHUNK, down)
        share((0, 1), row, CHUNK)

    def from_over(q):
        row = q * CHUNK
        for dz in (0, 3, 1):
            arrived(("y", dz, q), panel(dz, 1), row, CHUNK)
            share((dz, 1), row, CHUNK)
        for half in (0, HALF):
            arrived(("y", 2, q, half), panel(2, 1), row + half, HALF)
            share((2, 1), row + half, HALF)

    own_chunk(0)
    own_chunk(1)
    near(0, 0)
    own_chunk(3)
    own_chunk(2)
    partner(1)
    near(0, 1)
    far(0, 0)
    near(0, 3)
    partner(2)
    near(0, 2)
    far(0, 1)
    far(0, 3)
    near(1, 1)
    from_over(0)
    far(0, 2)
    near(1, 2)
    far(1, 1)
    from_over(3)
    far(1, 2)

    for name, (dz, dh), row, rows in shared:
        arrived(name, panel(dz, dh, 1), row, rows)
    for copy in sends:
        copy.wait_send()


def exchange(pieces):
    many = 128
    anywhere = pl.BlockSpec(memory_space=pl.ANY)
    return pl.pallas_call(
        exchange_kernel,
        out_shape=jax.ShapeDtypeStruct((PANELS * BLOCK, 128), BF16),
        in_specs=[anywhere],
        out_specs=anywhere,
        scratch_shapes=[
            pltpu.SemaphoreType.DMA((many,)),
            pltpu.SemaphoreType.DMA((many,)),
            pltpu.SemaphoreType.DMA,
        ],
        compiler_params=pltpu.CompilerParams(collective_id=0, has_side_effects=True),
        name="exchange",
    )(pieces)


LOADS = 8
UNIT = 2 * 2 * PER


def correlate_kernel(place, spectra, out, raw, wide, sorted_, ordered, sems):
    ch = pl.program_id(0)

    @pl.when(ch == 0)
    def _():
        part = PANELS * BLOCK // LOADS

        def load(j):
            rows = pl.ds(j * part, part)
            return pltpu.make_async_copy(spectra.at[rows], raw.at[rows], sems.at[j])

        for j in range(LOADS):
            load(j).start()
        for j in range(LOADS):
            load(j).wait()

            def widen(i, _):
                rows = pl.ds(pl.multiple_of(j * part + i * 256, 256), 256)
                wide[rows, :] = raw[rows, :].astype(F32)
                return 0

            lax.fori_loop(0, part // 256, widen, 0)

        def sort(b, _):
            for n in range(64):
                row = pl.multiple_of(place[b * 64 + n], 8)
                sorted_[n * UNIT : (n + 1) * UNIT, :] = wide[pl.ds(row, UNIT), :]
            rows = pl.ds(pl.multiple_of(b * 128, 128), 128)
            for e in range(2 * PER):
                ordered[e, rows, :] = sorted_[pl.ds(e, 128, stride=2 * PER), :].astype(BF16)
            return 0

        lax.fori_loop(0, STATIONS // 64, sort, 0)

    first = pl.multiple_of(lax.axis_index("panel") * 128, 128)
    lre, lim = ordered[ch, pl.ds(first, 128), :], ordered[PER + ch, pl.ds(first, 128), :]
    left = jnp.concatenate(
        [jnp.concatenate([lre, lim], axis=1), jnp.concatenate([lim, -lre], axis=1)], axis=0
    )
    for b in range(8):
        rows = pl.ds(b * 256, 256)
        right = jnp.concatenate([ordered[ch, rows, :], ordered[PER + ch, rows, :]], axis=1)
        prod = lax.dot_general(left, right, NT, preferred_element_type=F32) * (1.0 / FRAMES)
        out[0, 0, :, rows] = prod[:128].astype(BF16)
        out[1, 0, :, rows] = prod[128:].astype(BF16)


def correlate(place, spectra):
    return pl.pallas_call(
        correlate_kernel,
        grid=(PER,),
        out_shape=jax.ShapeDtypeStruct((2, PER, 128, INPUTS), BF16),
        in_specs=[pl.BlockSpec(memory_space=pltpu.SMEM), pl.BlockSpec(memory_space=pl.ANY)],
        out_specs=pl.BlockSpec((2, 1, 128, INPUTS), lambda i: (0, i, 0, 0)),
        scratch_shapes=[
            pltpu.VMEM((PANELS * BLOCK, 128), BF16),
            pltpu.VMEM((PANELS * BLOCK, 128), F32),
            pltpu.VMEM((64 * UNIT, 128), F32),
            pltpu.VMEM((2 * PER, INPUTS, 128), BF16),
            pltpu.SemaphoreType.DMA((LOADS,)),
        ],
        compiler_params=pltpu.CompilerParams(vmem_limit_bytes=56 * 2**20),
        cost_estimate=pl.CostEstimate(flops=2 * 6 * 256 * 2048 * 256, bytes_accessed=13 * 2**20, transcendentals=0),
        name="correlate",
    )(place, spectra)


def local(voltages, prototype, complex_gains, flagged, station_order):
    c = lax.axis_index("chan")
    keep = jnp.repeat(1.0 - flagged.astype(F32), 2)
    gains = (complex_gains * keep[:, None]).T.reshape(GROUPS, PER, 2, LOCAL)
    gains = jnp.pad(gains, ((0, 0), (0, 8 - PER), (0, 0), (0, 0)))
    gre, gim = gains[:, :, 0].reshape(GROUPS * 8, LOCAL), gains[:, :, 1].reshape(GROUPS * 8, LOCAL)
    dev = station_order // (LOCAL // 2)
    cs, ps = dev // PANELS, dev % PANELS
    r = ((cs // 2 - c // 2 + 4) % 4) * 2 + (cs % 2 + c % 2) % 2
    place = ((ps * 8 + r) * (LOCAL // 2) + station_order % (LOCAL // 2)) * UNIT
    pieces = channelize(voltages, prototype, gre, gim)
    spectra = exchange(pieces)
    return correlate(place, spectra)


def solution(mesh):
    placed = (
        P(("chan", "panel"), None),
        P(),
        P(("chan", "panel"), None),
        P(("chan", "panel")),
        P(),
    )
    return jax.shard_map(
        local, mesh=mesh, in_specs=placed, out_specs=P(None, "chan", "panel", None), check_vma=False
    )
```

```python
import functools
import math

import jax
import jax.numpy as jnp
import numpy as np
from jax import lax
from jax.experimental import pallas as pl
from jax.experimental.pallas import tpu as pltpu
from jax.sharding import PartitionSpec as P

MESH = pl.DeviceIdType.MESH
F32, BF16 = jnp.float32, jnp.bfloat16
NT = (((1,), (1,)), ((), ()))

NFFT, TAPS, FRAMES, NCHAN = 4096, 4, 128, 48
INPUTS, STATIONS = 2048, 1024
LOCAL = 16
GROUPS, PER = 8, 6
FALL = FRAMES + TAPS - 1
HALF_IN = LOCAL // 2
PIECE = HALF_IN * 2 * PER
HALF_ROWS = GROUPS * PIECE
BLOCK = 2 * HALF_ROWS
PANELS = 16


def table_rows():
    n = np.arange(NFFT)[None, :]
    j = np.arange(NCHAN)[:, None]
    m = (n * (NFFT // 4 + j)) % NFFT
    phase = m.astype(np.float32) * np.float32(2.0 * math.pi / NFFT)
    both = np.stack([np.cos(phase), -np.sin(phase)], axis=1)
    both = both.reshape(GROUPS, PER, 2, NFFT).transpose(0, 2, 1, 3)
    both = np.pad(both, ((0, 0), (0, 0), (0, 8 - PER), (0, 0)))
    return both.reshape(128, NFFT).astype(jnp.bfloat16)


STEP_F = 34
STARTS = (0, 34, 66, 97)
VOLT_COPIES = 8

CHUNK = BLOCK // 4
HALF = CHUNK // 2
Z_FIRST = (0, 1)
EVENTS = (
    ("own", 0, 0),
    ("own", 0, 1),
    ("near_up", 0, 0),
    ("near_down", 0, 0),
    ("over0", 1, 0),
    ("near_up", 0, 1),
    ("near_down", 0, 1),
    ("over0", 1, 1),
    ("own", 0, 2),
    ("far_up", 0, 0),
    ("far_down", 0, 0),
    ("partner", 1, 2),
    ("over3", 1, 0),
    ("own", 0, 3),
    ("partner", 1, 3),
    ("far_up", 0, 1),
    ("far_down", 0, 1),
    ("over1", 1, 0),
    ("near_up", 0, 2),
    ("near_down", 0, 2),
    ("over3", 1, 1),
    ("near_up", 1, 2),
    ("near_down", 1, 2),
    ("over1", 1, 1),
    ("near_up", 0, 3),
    ("near_down", 0, 3),
    ("over2a", 1, 0),
    ("over2b", 1, 0),
    ("near_up", 1, 3),
    ("near_down", 1, 3),
    ("over2a", 1, 1),
    ("far_up", 0, 2),
    ("far_down", 0, 2),
    ("over2b", 1, 1),
    ("far_up", 1, 2),
    ("far_down", 1, 2),
    ("far_up", 0, 3),
    ("far_down", 0, 3),
    ("far_up", 1, 3),
    ("far_down", 1, 3),
)


def spectra_kernel(
    volt, proto, table, gains, flagged, order, out, place,
    buf, w, y, s, half0, half1, gt, gre, gim, vs, ss, rs, own_sem,
):
    c, p = lax.axis_index("chan"), lax.axis_index("panel")
    x, yl = c // 2, c % 2
    z, h, k = p // 4, (p // 2) % 2, p % 2

    def panel(dz, dh, dk=0):
        return ((z + dz) % 4) * 4 + ((h + dh) % 2) * 2 + (k + dk) % 2

    def at_panel(pan):
        return {"chan": c, "panel": pan}

    def chan_target(r):
        return ((x + 4 - r // 2) % 4) * 2 + (yl + r % 2) % 2

    up, down, over, sib = (at_panel(a) for a in (panel(1, 0), panel(3, 0), panel(0, 1), panel(0, 0, 1)))

    per = -(-FALL // VOLT_COPIES)
    cuts = [(a, min(per, FALL - a)) for a in range(0, FALL, per)]

    def load(i):
        cols = pl.ds(cuts[i][0] * NFFT, cuts[i][1] * NFFT)
        return pltpu.make_async_copy(volt.at[:, cols], buf.at[:, cols], vs.at[i])

    for i in range(len(cuts)):
        load(i).start()

    barrier = pltpu.get_barrier_semaphore()
    greet = [{"chan": chan_target(r), "panel": q} for r in range(1, GROUPS) for q in (p, panel(0, 1))]
    greet += [up, down, over, sib]
    for d in greet:
        pl.semaphore_signal(barrier, inc=1, device_id=d, device_id_type=MESH)

    tab = 512

    def weights(i, _):
        cols = pl.ds(pl.multiple_of(i * tab, tab), tab)
        t = table[:, cols].astype(F32)
        for tap in range(TAPS):
            w[pl.ds(tap * 128, 128), cols] = (t * proto[tap : tap + 1, cols]).astype(BF16)
        return 0

    lax.fori_loop(0, NFFT // tab, weights, 0)

    gt[...] = jnp.zeros_like(gt)
    gt[:LOCAL, : 2 * NCHAN] = gains[...]
    gt[...] = gt[...].T
    gre[...] = jnp.zeros_like(gre)
    gim[...] = jnp.zeros_like(gim)
    for g in range(GROUPS):
        gre[g * 8 : g * 8 + PER, :] = gt[pl.ds(g * 2 * PER, PER, stride=2), :]
        gim[g * 8 : g * 8 + PER, :] = gt[pl.ds(g * 2 * PER + 1, PER, stride=2), :]

    st = order[...]
    dev, within = st // HALF_IN, st % HALF_IN
    cs, ps = dev // PANELS, dev % PANELS
    r = ((cs // 2 - x + 4) % 4) * 2 + (cs % 2 + yl) % 2
    place[...] = ((ps * 2 + within // 4) * GROUPS + r) * PIECE + (within % 4) * (4 * PER)

    waited = [0]

    def channelize(hh, dest):
        low = hh * HALF_IN
        for first in STARTS:
            while waited[0] < len(cuts) and cuts[waited[0]][0] < first + STEP_F:
                load(waited[0]).wait()
                waited[0] += 1
            v = jnp.concatenate(
                [buf[low : low + HALF_IN, pl.ds((first + f) * NFFT, NFFT)] for f in range(STEP_F)], axis=0
            )
            rows = pl.ds(first * HALF_IN, STEP_F * HALF_IN)
            for j in range(2):
                prod = lax.dot_general(v, w[pl.ds(j * 256, 256), :], NT, preferred_element_type=F32)
                y[2 * j, rows, :] = prod[:, :128]
                y[2 * j + 1, rows, :] = prod[:, 128:]
        for i in range(HALF_IN):
            raw = y[0, pl.ds(i, FRAMES, stride=HALF_IN), :]
            for t in range(1, TAPS):
                raw = raw + y[t, pl.ds(t * HALF_IN + i, FRAMES, stride=HALF_IN), :]
            turned = raw.T
            n = low + i
            keep = (1 - flagged[n // 2]).astype(F32)
            for g in range(GROUPS):
                re, im = turned[g * 16 : g * 16 + 8], turned[g * 16 + 8 : g * 16 + 16]
                a, b = gre[g * 8 : g * 8 + 8, n : n + 1] * keep, gim[g * 8 : g * 8 + 8, n : n + 1] * keep
                at = g * PIECE + i * 2 * PER
                s[at : at + PER, :] = (a * re - b * im)[:PER]
                s[at + PER : at + 2 * PER, :] = (a * im + b * re)[:PER]
        dest[...] = s[...].astype(BF16)

    ids, sends = {}, []

    def number(name):
        return ids.setdefault(name, len(ids))

    def region(block, row, rows):
        return out.at[pl.ds(pl.multiple_of(block * BLOCK + row, 16), rows)]

    def send(name, block, row, rows, device, source=None):
        n = number(name)
        there = region(block, row, rows)
        copy = pltpu.make_async_remote_copy(
            there if source is None else source, there, ss.at[n], rs.at[n], device_id=device, device_id_type=MESH
        )
        copy.start()
        sends.append(copy)

    def arrived(name, block, row, rows):
        n = number(name)
        here = region(block, row, rows)
        pltpu.make_async_remote_copy(here, here, ss.at[n], rs.at[n], device_id=sib, device_id_type=MESH).wait_recv()

    mine = panel(0, 0)

    def turn(hh, src):
        row = hh * HALF_ROWS
        pltpu.make_async_copy(
            src.at[pl.ds(pl.multiple_of(c * PIECE, 16), PIECE)], region(mine, row, PIECE), own_sem.at[hh]
        ).start()
        for r in (0, 1, 2, 3, 6, 7, 4, 5):
            t = chan_target(r)
            piece = src.at[pl.ds(pl.multiple_of(t * PIECE, 16), PIECE)]
            if r:
                send(("a", hh, r), mine, row + r * PIECE, PIECE, {"chan": t, "panel": p}, piece)
            if hh * 2 + r // 4 not in Z_FIRST:
                send(("b", hh, r), mine, row + r * PIECE, PIECE, {"chan": t, "panel": panel(0, 1)}, piece)

    shared = []

    def share(place_of, row, rows):
        name = ("s", place_of, row)
        send(name, panel(*place_of), row, rows, sib)
        shared.append((name, place_of, row, rows))

    def pass_on(what, dh, q):
        row, hh = q * CHUNK, q // 2
        z_first = q in Z_FIRST
        if what in ("own", "partner"):
            block = panel(0, dh)
            for r in range(4 * (q % 2), 4 * (q % 2) + 4):
                at = hh * HALF_ROWS + r * PIECE
                if what == "own" and r == 0:
                    here = region(block, at, PIECE)
                    pltpu.make_async_copy(here, here, own_sem.at[hh]).wait()
                else:
                    arrived(("a" if what == "own" else "b", hh, r), block, at, PIECE)
            send(("up", dh, q), block, row, CHUNK, up)
            send(("down", dh, q), block, row, CHUNK, down)
            if z_first:
                send(("y", 0, q), block, row, CHUNK, over)
            share((0, dh), row, CHUNK)
        elif what in ("near_up", "near_down"):
            dz, way, half = (3, up, 0) if what == "near_up" else (1, down, HALF)
            block = panel(dz, dh)
            arrived((what[5:], dh, q), block, row, CHUNK)
            send(("far_" + what[5:], dh, q), block, row + half, HALF, way)
            if z_first:
                send(("y", dz, q), block, row, CHUNK, over)
            share((dz, dh), row, CHUNK)
        elif what in ("far_up", "far_down"):
            at = row + (0 if what == "far_up" else HALF)
            arrived((what, dh, q), panel(2, dh), at, HALF)
            if z_first:
                send(("y2", at), panel(2, dh), at, HALF, over)
            share((2, dh), at, HALF)
        elif what in ("over2a", "over2b"):
            at = row + (0 if what == "over2a" else HALF)
            arrived(("y2", at), panel(2, 1), at, HALF)
            share((2, 1), at, HALF)
        else:
            dz = int(what[4])
            arrived(("y", dz, q), panel(dz, 1), row, CHUNK)
            share((dz, 1), row, CHUNK)

    channelize(0, half0)
    pl.semaphore_wait(barrier, len(greet))
    turn(0, half0)
    channelize(1, half1)
    turn(1, half1)
    for event in EVENTS:
        pass_on(*event)
    for name, (dz, dh), row, rows in shared:
        arrived(name, panel(dz, dh, 1), row, rows)
    for copy in sends:
        copy.wait_send()


def spectra_of_all(volt, proto, gains, flagged, order):
    vm, sm = pl.BlockSpec(memory_space=pltpu.VMEM), pl.BlockSpec(memory_space=pltpu.SMEM)
    anywhere = pl.BlockSpec(memory_space=pl.ANY)
    many = 160
    return pl.pallas_call(
        spectra_kernel,
        out_shape=(
            jax.ShapeDtypeStruct((PANELS * BLOCK, 128), BF16),
            jax.ShapeDtypeStruct((8, 128), jnp.int32),
        ),
        in_specs=[anywhere, vm, vm, vm, sm, vm],
        out_specs=(anywhere, vm),
        scratch_shapes=[
            pltpu.VMEM((LOCAL, FALL * NFFT), BF16),
            pltpu.VMEM((TAPS * 128, NFFT), BF16),
            pltpu.VMEM((TAPS, FALL * HALF_IN, 128), F32),
            pltpu.VMEM((HALF_ROWS, 128), F32),
            pltpu.VMEM((HALF_ROWS, 128), BF16),
            pltpu.VMEM((HALF_ROWS, 128), BF16),
            pltpu.VMEM((128, 128), F32),
            pltpu.VMEM((GROUPS * 8, 128), F32),
            pltpu.VMEM((GROUPS * 8, 128), F32),
            pltpu.SemaphoreType.DMA((VOLT_COPIES,)),
            pltpu.SemaphoreType.DMA((many,)),
            pltpu.SemaphoreType.DMA((many,)),
            pltpu.SemaphoreType.DMA((2,)),
        ],
        compiler_params=pltpu.CompilerParams(
            collective_id=0, has_side_effects=True, vmem_limit_bytes=56 * 2**20
        ),
        name="spectra",
    )(volt, proto, jnp.asarray(table_rows()), gains, flagged, order)


LOADS = 8
UNIT = 2 * 2 * PER


def correlate_kernel(place, spectra, out, raw, wide, sorted_, ordered, sems):
    ch = pl.program_id(0)

    @pl.when(ch == 0)
    def _():
        part = PANELS * BLOCK // LOADS

        def load(j):
            rows = pl.ds(j * part, part)
            return pltpu.make_async_copy(spectra.at[rows], raw.at[rows], sems.at[j])

        for j in range(LOADS):
            load(j).start()
        for j in range(LOADS):
            load(j).wait()

            def widen(i, _):
                rows = pl.ds(pl.multiple_of(j * part + i * 256, 256), 256)
                wide[rows, :] = raw[rows, :].astype(F32)
                return 0

            lax.fori_loop(0, part // 256, widen, 0)

        def sort(b, _):
            for n in range(64):
                row = pl.multiple_of(place[b // 2, (b % 2) * 64 + n], 8)
                sorted_[n * UNIT : (n + 1) * UNIT, :] = wide[pl.ds(row, UNIT), :]
            rows = pl.ds(pl.multiple_of(b * 128, 128), 128)
            for e in range(2 * PER):
                ordered[e, rows, :] = sorted_[pl.ds(e, 128, stride=2 * PER), :].astype(BF16)
            return 0

        lax.fori_loop(0, STATIONS // 64, sort, 0)

    first = pl.multiple_of(lax.axis_index("panel") * 128, 128)
    lre, lim = ordered[ch, pl.ds(first, 128), :], ordered[PER + ch, pl.ds(first, 128), :]
    left = jnp.concatenate(
        [jnp.concatenate([lre, lim], axis=1), jnp.concatenate([lim, -lre], axis=1)], axis=0
    )
    for b in range(8):
        rows = pl.ds(b * 256, 256)
        right = jnp.concatenate([ordered[ch, rows, :], ordered[PER + ch, rows, :]], axis=1)
        prod = lax.dot_general(left, right, NT, preferred_element_type=F32) * (1.0 / FRAMES)
        out[0, 0, :, rows] = prod[:128].astype(BF16)
        out[1, 0, :, rows] = prod[128:].astype(BF16)


def correlate(place, spectra):
    return pl.pallas_call(
        correlate_kernel,
        grid=(PER,),
        out_shape=jax.ShapeDtypeStruct((2, PER, 128, INPUTS), BF16),
        in_specs=[pl.BlockSpec(memory_space=pltpu.SMEM), pl.BlockSpec(memory_space=pl.ANY)],
        out_specs=pl.BlockSpec((2, 1, 128, INPUTS), lambda i: (0, i, 0, 0)),
        scratch_shapes=[
            pltpu.VMEM((PANELS * BLOCK, 128), BF16),
            pltpu.VMEM((PANELS * BLOCK, 128), F32),
            pltpu.VMEM((64 * UNIT, 128), F32),
            pltpu.VMEM((2 * PER, INPUTS, 128), BF16),
            pltpu.SemaphoreType.DMA((LOADS,)),
        ],
        compiler_params=pltpu.CompilerParams(vmem_limit_bytes=56 * 2**20),
        cost_estimate=pl.CostEstimate(flops=2 * 6 * 256 * 2048 * 256, bytes_accessed=13 * 2**20, transcendentals=0),
        name="correlate",
    )(place, spectra)


def local(voltages, prototype, complex_gains, flagged, station_order):
    spectra, place = spectra_of_all(
        voltages, prototype, complex_gains, flagged, station_order.reshape(8, 128)
    )
    return correlate(place, spectra)


def solution(mesh):
    placed = (
        P(("chan", "panel"), None),
        P(),
        P(("chan", "panel"), None),
        P(("chan", "panel")),
        P(),
    )
    return jax.shard_map(
        local, mesh=mesh, in_specs=placed, out_specs=P(None, "chan", "panel", None), check_vma=False
    )
```

```python
import functools
import math

import jax
import jax.numpy as jnp
import numpy as np
from jax import lax
from jax.experimental import pallas as pl
from jax.experimental.pallas import tpu as pltpu
from jax.sharding import PartitionSpec as P

MESH = pl.DeviceIdType.MESH
F32, BF16 = jnp.float32, jnp.bfloat16
NT = (((1,), (1,)), ((), ()))

NFFT, TAPS, FRAMES, NCHAN = 4096, 4, 128, 48
INPUTS, STATIONS = 2048, 1024
LOCAL = 16
GROUPS, PER = 8, 6
FALL = FRAMES + TAPS - 1
HALF_IN = LOCAL // 2
PIECE = HALF_IN * 2 * PER
HALF_ROWS = GROUPS * PIECE
BLOCK = 2 * HALF_ROWS
PANELS = 16


def table_rows():
    n = np.arange(NFFT)[None, :]
    j = np.arange(NCHAN)[:, None]
    m = (n * (NFFT // 4 + j)) % NFFT
    phase = m.astype(np.float32) * np.float32(2.0 * math.pi / NFFT)
    both = np.stack([np.cos(phase), -np.sin(phase)], axis=1)
    both = both.reshape(GROUPS, PER, 2, NFFT).transpose(0, 2, 1, 3)
    both = np.pad(both, ((0, 0), (0, 0), (0, 8 - PER), (0, 0)))
    return both.reshape(128, NFFT).astype(jnp.bfloat16)


RECEIVES = 41
STEP_F = 34
STARTS = (0, 34, 66, 97)
VOLT_COPIES = 8

CHUNK = BLOCK // 4
HALF = CHUNK // 2
Z_FIRST = (0, 1)
EVENTS = (
    ("own", 0, 0),
    ("own", 0, 1),
    ("near_up", 0, 0),
    ("near_down", 0, 0),
    ("over0", 1, 0),
    ("near_up", 0, 1),
    ("near_down", 0, 1),
    ("over0", 1, 1),
    ("own", 0, 2),
    ("far_up", 0, 0),
    ("far_down", 0, 0),
    ("partner", 1, 2),
    ("over3", 1, 0),
    ("own", 0, 3),
    ("partner", 1, 3),
    ("far_up", 0, 1),
    ("far_down", 0, 1),
    ("over1", 1, 0),
    ("near_up", 0, 2),
    ("near_down", 0, 2),
    ("over3", 1, 1),
    ("near_up", 1, 2),
    ("near_down", 1, 2),
    ("over1", 1, 1),
    ("near_up", 0, 3),
    ("near_down", 0, 3),
    ("over2a", 1, 0),
    ("over2b", 1, 0),
    ("near_up", 1, 3),
    ("near_down", 1, 3),
    ("over2a", 1, 1),
    ("far_up", 0, 2),
    ("far_down", 0, 2),
    ("over2b", 1, 1),
    ("far_up", 1, 2),
    ("far_down", 1, 2),
    ("far_up", 0, 3),
    ("far_down", 0, 3),
    ("far_up", 1, 3),
    ("far_down", 1, 3),
)


def spectra_kernel(
    volt, proto, table, gains, flagged, order, out, place,
    buf, w, y, s, half0, half1, gt, gre, gim, vs, ss, rs, own_sem,
):
    c, p = lax.axis_index("chan"), lax.axis_index("panel")
    x, yl = c // 2, c % 2
    z, h, k = p // 4, (p // 2) % 2, p % 2

    def panel(dz, dh, dk=0):
        return ((z + dz) % 4) * 4 + ((h + dh) % 2) * 2 + (k + dk) % 2

    def at_panel(pan):
        return {"chan": c, "panel": pan}

    def chan_target(r):
        return ((x + 4 - r // 2) % 4) * 2 + (yl + r % 2) % 2

    up, down, over, sib = (at_panel(a) for a in (panel(1, 0), panel(3, 0), panel(0, 1), panel(0, 0, 1)))

    per = -(-FALL // VOLT_COPIES)
    cuts = [(a, min(per, FALL - a)) for a in range(0, FALL, per)]

    def load(i):
        cols = pl.ds(cuts[i][0] * NFFT, cuts[i][1] * NFFT)
        return pltpu.make_async_copy(volt.at[:, cols], buf.at[:, cols], vs.at[i])

    for i in range(len(cuts)):
        load(i).start()

    barrier = pltpu.get_barrier_semaphore()
    greet = [{"chan": chan_target(r), "panel": q} for r in range(1, GROUPS) for q in (p, panel(0, 1))]
    greet += [up, down, over, sib]
    for d in greet:
        pl.semaphore_signal(barrier, inc=1, device_id=d, device_id_type=MESH)

    tab = 512

    def weights(i, _):
        cols = pl.ds(pl.multiple_of(i * tab, tab), tab)
        t = table[:, cols].astype(F32)
        for tap in range(TAPS):
            w[pl.ds(tap * 128, 128), cols] = (t * proto[tap : tap + 1, cols]).astype(BF16)
        return 0

    lax.fori_loop(0, NFFT // tab, weights, 0)

    gt[...] = jnp.zeros_like(gt)
    gt[:LOCAL, : 2 * NCHAN] = gains[...]
    gt[...] = gt[...].T
    gre[...] = jnp.zeros_like(gre)
    gim[...] = jnp.zeros_like(gim)
    for g in range(GROUPS):
        gre[g * 8 : g * 8 + PER, :] = gt[pl.ds(g * 2 * PER, PER, stride=2), :]
        gim[g * 8 : g * 8 + PER, :] = gt[pl.ds(g * 2 * PER + 1, PER, stride=2), :]

    st = order[...]
    dev, within = st // HALF_IN, st % HALF_IN
    cs, ps = dev // PANELS, dev % PANELS
    r = ((cs // 2 - x + 4) % 4) * 2 + (cs % 2 + yl) % 2
    place[...] = ((ps * 2 + within // 4) * GROUPS + r) * PIECE + (within % 4) * (4 * PER)

    waited = [0]

    def channelize(hh, dest):
        low = hh * HALF_IN
        for first in STARTS:
            while waited[0] < len(cuts) and cuts[waited[0]][0] < first + STEP_F:
                load(waited[0]).wait()
                waited[0] += 1
            v = jnp.concatenate(
                [buf[low : low + HALF_IN, pl.ds((first + f) * NFFT, NFFT)] for f in range(STEP_F)], axis=0
            )
            rows = pl.ds(first * HALF_IN, STEP_F * HALF_IN)
            for j in range(2):
                prod = lax.dot_general(v, w[pl.ds(j * 256, 256), :], NT, preferred_element_type=F32)
                y[2 * j, rows, :] = prod[:, :128]
                y[2 * j + 1, rows, :] = prod[:, 128:]
        for i in range(HALF_IN):
            raw = y[0, pl.ds(i, FRAMES, stride=HALF_IN), :]
            for t in range(1, TAPS):
                raw = raw + y[t, pl.ds(t * HALF_IN + i, FRAMES, stride=HALF_IN), :]
            turned = raw.T
            n = low + i
            keep = (1 - flagged[n // 2]).astype(F32)
            for g in range(GROUPS):
                re, im = turned[g * 16 : g * 16 + 8], turned[g * 16 + 8 : g * 16 + 16]
                a, b = gre[g * 8 : g * 8 + 8, n : n + 1] * keep, gim[g * 8 : g * 8 + 8, n : n + 1] * keep
                at = g * PIECE + i * 2 * PER
                s[at : at + PER, :] = (a * re - b * im)[:PER]
                s[at + PER : at + 2 * PER, :] = (a * im + b * re)[:PER]
        dest[...] = s[...].astype(BF16)

    ids, sends = {}, []

    def number(name):
        return ids.setdefault(name, len(ids))

    def region(block, row, rows):
        return out.at[pl.ds(pl.multiple_of(block * BLOCK + row, 16), rows)]

    def send(name, block, row, rows, device, source=None):
        n = number(name)
        there = region(block, row, rows)
        copy = pltpu.make_async_remote_copy(
            there if source is None else source, there, ss, rs.at[n], device_id=device, device_id_type=MESH
        )
        copy.start()
        sends.append(rows)

    def arrived(name, block, row, rows):
        n = number(name)
        here = region(block, row, rows)
        pltpu.make_async_remote_copy(here, here, ss, rs.at[n], device_id=sib, device_id_type=MESH).wait_recv()

    mine = panel(0, 0)

    def turn(hh, src):
        row = hh * HALF_ROWS
        pltpu.make_async_copy(
            src.at[pl.ds(pl.multiple_of(c * PIECE, 16), PIECE)], region(mine, row, PIECE), own_sem.at[hh]
        ).start()
        for r in (0, 1, 2, 3, 6, 7, 4, 5):
            t = chan_target(r)
            piece = src.at[pl.ds(pl.multiple_of(t * PIECE, 16), PIECE)]
            if r:
                send(("a", hh * 2 + r // 4), mine, row + r * PIECE, PIECE, {"chan": t, "panel": p}, piece)
            if hh * 2 + r // 4 not in Z_FIRST:
                send(("b", hh * 2 + r // 4), mine, row + r * PIECE, PIECE, {"chan": t, "panel": panel(0, 1)}, piece)

    shared = []

    def share(place_of, row, rows):
        send("share", panel(*place_of), row, rows, sib)
        shared.append(rows)

    def pass_on(what, dh, q):
        row, hh = q * CHUNK, q // 2
        z_first = q in Z_FIRST
        if what in ("own", "partner"):
            block = panel(0, dh)
            skip = 0
            if what == "own" and q % 2 == 0:
                skip = PIECE
                here = region(block, row, PIECE)
                pltpu.make_async_copy(here, here, own_sem.at[hh]).wait()
            arrived(("a" if what == "own" else "b", q), block, row + skip, CHUNK - skip)
            send(("up", dh, q), block, row, CHUNK, up)
            send(("down", dh, q), block, row, CHUNK, down)
            if z_first:
                send(("y", 0, q), block, row, CHUNK, over)
            share((0, dh), row, CHUNK)
        elif what in ("near_up", "near_down"):
            dz, way, half = (3, up, 0) if what == "near_up" else (1, down, HALF)
            block = panel(dz, dh)
            arrived((what[5:], dh, q), block, row, CHUNK)
            send(("far_" + what[5:], dh, q), block, row + half, HALF, way)
            if z_first:
                send(("y", dz, q), block, row, CHUNK, over)
            share((dz, dh), row, CHUNK)
        elif what in ("far_up", "far_down"):
            at = row + (0 if what == "far_up" else HALF)
            arrived((what, dh, q), panel(2, dh), at, HALF)
            if z_first:
                send(("y2", at), panel(2, dh), at, HALF, over)
            share((2, dh), at, HALF)
        elif what in ("over2a", "over2b"):
            at = row + (0 if what == "over2a" else HALF)
            arrived(("y2", at), panel(2, 1), at, HALF)
            share((2, 1), at, HALF)
        else:
            dz = int(what[4])
            arrived(("y", dz, q), panel(dz, 1), row, CHUNK)
            share((dz, 1), row, CHUNK)

    channelize(0, half0)
    pl.semaphore_wait(barrier, len(greet))
    turn(0, half0)
    channelize(1, half1)
    turn(1, half1)
    for event in EVENTS:
        pass_on(*event)
    arrived("share", 0, 0, sum(shared))
    gone = out.at[pl.ds(0, sum(sends))]
    pltpu.make_async_remote_copy(gone, gone, ss, rs.at[0], device_id=sib, device_id_type=MESH).wait_send()


def spectra_of_all(volt, proto, gains, flagged, order):
    vm, sm = pl.BlockSpec(memory_space=pltpu.VMEM), pl.BlockSpec(memory_space=pltpu.SMEM)
    anywhere = pl.BlockSpec(memory_space=pl.ANY)
    return pl.pallas_call(
        spectra_kernel,
        out_shape=(
            jax.ShapeDtypeStruct((PANELS * BLOCK, 128), BF16),
            jax.ShapeDtypeStruct((8, 128), jnp.int32),
        ),
        in_specs=[anywhere, vm, vm, vm, sm, vm],
        out_specs=(anywhere, vm),
        scratch_shapes=[
            pltpu.VMEM((LOCAL, FALL * NFFT), BF16),
            pltpu.VMEM((TAPS * 128, NFFT), BF16),
            pltpu.VMEM((TAPS, FALL * HALF_IN, 128), F32),
            pltpu.VMEM((HALF_ROWS, 128), F32),
            pltpu.VMEM((HALF_ROWS, 128), BF16),
            pltpu.VMEM((HALF_ROWS, 128), BF16),
            pltpu.VMEM((128, 128), F32),
            pltpu.VMEM((GROUPS * 8, 128), F32),
            pltpu.VMEM((GROUPS * 8, 128), F32),
            pltpu.SemaphoreType.DMA((VOLT_COPIES,)),
            pltpu.SemaphoreType.DMA,
            pltpu.SemaphoreType.DMA((RECEIVES,)),
            pltpu.SemaphoreType.DMA((2,)),
        ],
        compiler_params=pltpu.CompilerParams(
            collective_id=0, has_side_effects=True, vmem_limit_bytes=56 * 2**20
        ),
        name="spectra",
    )(volt, proto, jnp.asarray(table_rows()), gains, flagged, order)


LOADS = 8
UNIT = 2 * 2 * PER


WIDTH = 256
COLUMNS = INPUTS // WIDTH


def correlate_kernel(place, spectra, out, raw, wide, sorted_, left, result, sems, out_sems):
    part = PANELS * BLOCK // LOADS

    def load(j):
        rows = pl.ds(j * part, part)
        return pltpu.make_async_copy(spectra.at[rows], raw.at[rows], sems.at[j])

    for j in range(LOADS):
        load(j).start()
    for j in range(LOADS):
        load(j).wait()

        def widen(i, _):
            rows = pl.ds(pl.multiple_of(j * part + i * 256, 256), 256)
            wide[rows, :] = raw[rows, :].astype(F32)
            return 0

        lax.fori_loop(0, part // 256, widen, 0)

    def sort(line, first, stations):
        for n in range(stations):
            row = pl.multiple_of(place[line, first + n], 8)
            sorted_[n * UNIT : (n + 1) * UNIT, :] = wide[pl.ds(row, UNIT), :]

    def part_of(e, rows):
        return sorted_[pl.ds(e, rows, stride=2 * PER), :].astype(BF16)

    p = lax.axis_index("panel")
    sort(p // 2, (p % 2) * 64, 64)
    for ch in range(PER):
        re, im = part_of(ch, 128), part_of(PER + ch, 128)
        left[ch, :128, :128] = re
        left[ch, :128, 128:] = im
        left[ch, 128:, :128] = im
        left[ch, 128:, 128:] = -re

    def write(b):
        columns = pl.ds(pl.multiple_of(b * WIDTH, WIDTH), WIDTH)
        return pltpu.make_async_copy(result.at[b], out.at[:, :, :, columns], out_sems.at[b])

    def block(b, _):
        sort(b, 0, WIDTH // 2)
        for ch in range(PER):
            right = jnp.concatenate([part_of(ch, WIDTH), part_of(PER + ch, WIDTH)], axis=1)
            prod = lax.dot_general(left[ch], right, NT, preferred_element_type=F32) * (1.0 / FRAMES)
            result[b, 0, ch] = prod[:128].astype(BF16)
            result[b, 1, ch] = prod[128:].astype(BF16)
        write(b).start()
        return 0

    lax.fori_loop(0, COLUMNS, block, 0)
    for b in range(COLUMNS):
        write(b).wait()


def correlate(place, spectra):
    return pl.pallas_call(
        correlate_kernel,
        out_shape=jax.ShapeDtypeStruct((2, PER, 128, INPUTS), BF16),
        in_specs=[pl.BlockSpec(memory_space=pltpu.SMEM), pl.BlockSpec(memory_space=pl.ANY)],
        out_specs=pl.BlockSpec(memory_space=pl.ANY),
        scratch_shapes=[
            pltpu.VMEM((PANELS * BLOCK, 128), BF16),
            pltpu.VMEM((PANELS * BLOCK, 128), F32),
            pltpu.VMEM((WIDTH // 2 * UNIT, 128), F32),
            pltpu.VMEM((PER, 256, 256), BF16),
            pltpu.VMEM((COLUMNS, 2, PER, 128, WIDTH), BF16),
            pltpu.SemaphoreType.DMA((LOADS,)),
            pltpu.SemaphoreType.DMA((COLUMNS,)),
        ],
        compiler_params=pltpu.CompilerParams(vmem_limit_bytes=56 * 2**20),
        cost_estimate=pl.CostEstimate(flops=2 * 6 * 256 * 2048 * 256, bytes_accessed=13 * 2**20, transcendentals=0),
        name="correlate",
    )(place, spectra)


def local(voltages, prototype, complex_gains, flagged, station_order):
    spectra, place = spectra_of_all(
        voltages, prototype, complex_gains, flagged, station_order.reshape(8, 128)
    )
    return correlate(place, spectra)


def solution(mesh):
    placed = (
        P(("chan", "panel"), None),
        P(),
        P(("chan", "panel"), None),
        P(("chan", "panel")),
        P(),
    )
    return jax.shard_map(
        local, mesh=mesh, in_specs=placed, out_specs=P(None, "chan", "panel", None), check_vma=False
    )
```

```python
import functools
import math

import jax
import jax.numpy as jnp
import numpy as np
from jax import lax
from jax.experimental import pallas as pl
from jax.experimental.pallas import tpu as pltpu
from jax.sharding import PartitionSpec as P

MESH = pl.DeviceIdType.MESH
F32, BF16 = jnp.float32, jnp.bfloat16
NT = (((1,), (1,)), ((), ()))

NFFT, TAPS, FRAMES, NCHAN = 4096, 4, 128, 48
INPUTS, STATIONS = 2048, 1024
LOCAL = 16
GROUPS, PER = 8, 6
FALL = FRAMES + TAPS - 1
HALF_IN = LOCAL // 2
PIECE = HALF_IN * 2 * PER
HALF_ROWS = GROUPS * PIECE
BLOCK = 2 * HALF_ROWS
PANELS = 16


def table_rows():
    n = np.arange(NFFT)[None, :]
    j = np.arange(NCHAN)[:, None]
    m = (n * (NFFT // 4 + j)) % NFFT
    phase = m.astype(np.float32) * np.float32(2.0 * math.pi / NFFT)
    both = np.stack([np.cos(phase), -np.sin(phase)], axis=1)
    both = both.reshape(GROUPS, PER, 2, NFFT).transpose(0, 2, 1, 3)
    both = np.pad(both, ((0, 0), (0, 0), (0, 8 - PER), (0, 0)))
    return both.reshape(128, NFFT).astype(jnp.bfloat16)


RECEIVES = 41
STEP_F = 34
STARTS = (0, 34, 66, 97)
VOLT_COPIES = 8

PER_HALF = 2
AT_ONCE = GROUPS // PER_HALF
CHUNK = HALF_ROWS // PER_HALF
HALF = CHUNK // 2
Z_FIRST = (0, 2)
EVENTS = (
    ("own", 0, 0),
    ("own", 0, 1),
    ("partner", 1, 1),
    ("near_up", 0, 0),
    ("near_down", 0, 0),
    ("over0", 1, 0),
    ("near_up", 0, 1),
    ("near_down", 0, 1),
    ("own", 0, 2),
    ("over3", 1, 0),
    ("near_up", 1, 1),
    ("near_down", 1, 1),
    ("own", 0, 3),
    ("partner", 1, 3),
    ("far_up", 0, 0),
    ("far_down", 0, 0),
    ("over1", 1, 0),
    ("far_up", 0, 1),
    ("far_down", 0, 1),
    ("over0", 1, 2),
    ("near_up", 0, 2),
    ("near_down", 0, 2),
    ("over2a", 1, 0),
    ("far_up", 1, 1),
    ("far_down", 1, 1),
    ("over2b", 1, 0),
    ("near_up", 0, 3),
    ("near_down", 0, 3),
    ("over3", 1, 2),
    ("near_up", 1, 3),
    ("near_down", 1, 3),
    ("over1", 1, 2),
    ("far_up", 0, 2),
    ("far_down", 0, 2),
    ("far_up", 0, 3),
    ("far_down", 0, 3),
    ("far_up", 1, 3),
    ("far_down", 1, 3),
    ("over2a", 1, 2),
    ("over2b", 1, 2),
)


def spectra_kernel(
    volt, proto, table, gains, flagged, order, out, place,
    buf, w, y, s, half0, half1, gt, gre, gim, vs, ss, rs, own_sem,
):
    c, p = lax.axis_index("chan"), lax.axis_index("panel")
    x, yl = c // 2, c % 2
    z, h, k = p // 4, (p // 2) % 2, p % 2

    def panel(dz, dh, dk=0):
        return ((z + dz) % 4) * 4 + ((h + dh) % 2) * 2 + (k + dk) % 2

    def at_panel(pan):
        return {"chan": c, "panel": pan}

    def chan_target(r):
        return ((x + 4 - r // 2) % 4) * 2 + (yl + r % 2) % 2

    up, down, over, sib = (at_panel(a) for a in (panel(1, 0), panel(3, 0), panel(0, 1), panel(0, 0, 1)))

    per = -(-FALL // VOLT_COPIES)
    cuts = [(a, min(per, FALL - a)) for a in range(0, FALL, per)]

    def load(i):
        cols = pl.ds(cuts[i][0] * NFFT, cuts[i][1] * NFFT)
        return pltpu.make_async_copy(volt.at[:, cols], buf.at[:, cols], vs.at[i])

    for i in range(len(cuts)):
        load(i).start()

    barrier = pltpu.get_barrier_semaphore()
    greet = [{"chan": chan_target(r), "panel": q} for r in range(1, GROUPS) for q in (p, panel(0, 1))]
    greet += [up, down, over, sib]
    for d in greet:
        pl.semaphore_signal(barrier, inc=1, device_id=d, device_id_type=MESH)

    tab = 512

    def weights(i, _):
        cols = pl.ds(pl.multiple_of(i * tab, tab), tab)
        t = table[:, cols].astype(F32)
        for tap in range(TAPS):
            w[pl.ds(tap * 128, 128), cols] = (t * proto[tap : tap + 1, cols]).astype(BF16)
        return 0

    lax.fori_loop(0, NFFT // tab, weights, 0)

    gt[...] = jnp.zeros_like(gt)
    gt[:LOCAL, : 2 * NCHAN] = gains[...]
    gt[...] = gt[...].T
    gre[...] = jnp.zeros_like(gre)
    gim[...] = jnp.zeros_like(gim)
    for g in range(GROUPS):
        gre[g * 8 : g * 8 + PER, :] = gt[pl.ds(g * 2 * PER, PER, stride=2), :]
        gim[g * 8 : g * 8 + PER, :] = gt[pl.ds(g * 2 * PER + 1, PER, stride=2), :]

    st = order[...]
    dev, within = st // HALF_IN, st % HALF_IN
    cs, ps = dev // PANELS, dev % PANELS
    r = ((cs // 2 - x + 4) % 4) * 2 + (cs % 2 + yl) % 2
    place[...] = ((ps * 2 + within // 4) * GROUPS + r) * PIECE + (within % 4) * (4 * PER)

    waited = [0]

    def channelize(hh, dest, between=None):
        low = hh * HALF_IN
        for first in STARTS:
            while waited[0] < len(cuts) and cuts[waited[0]][0] < first + STEP_F:
                load(waited[0]).wait()
                waited[0] += 1
            v = jnp.concatenate(
                [buf[low : low + HALF_IN, pl.ds((first + f) * NFFT, NFFT)] for f in range(STEP_F)], axis=0
            )
            rows = pl.ds(first * HALF_IN, STEP_F * HALF_IN)
            for j in range(2):
                prod = lax.dot_general(v, w[pl.ds(j * 256, 256), :], NT, preferred_element_type=F32)
                y[2 * j, rows, :] = prod[:, :128]
                y[2 * j + 1, rows, :] = prod[:, 128:]
        if between is not None:
            between()
        for i in range(HALF_IN):
            raw = y[0, pl.ds(i, FRAMES, stride=HALF_IN), :]
            for t in range(1, TAPS):
                raw = raw + y[t, pl.ds(t * HALF_IN + i, FRAMES, stride=HALF_IN), :]
            turned = raw.T
            n = low + i
            keep = (1 - flagged[n // 2]).astype(F32)
            for g in range(GROUPS):
                re, im = turned[g * 16 : g * 16 + 8], turned[g * 16 + 8 : g * 16 + 16]
                a, b = gre[g * 8 : g * 8 + 8, n : n + 1] * keep, gim[g * 8 : g * 8 + 8, n : n + 1] * keep
                at = g * PIECE + i * 2 * PER
                s[at : at + PER, :] = (a * re - b * im)[:PER]
                s[at + PER : at + 2 * PER, :] = (a * im + b * re)[:PER]
        dest[...] = s[...].astype(BF16)

    ids, sends = {}, []

    def number(name):
        return ids.setdefault(name, len(ids))

    def region(block, row, rows):
        return out.at[pl.ds(pl.multiple_of(block * BLOCK + row, 16), rows)]

    def send(name, block, row, rows, device, source=None):
        n = number(name)
        there = region(block, row, rows)
        copy = pltpu.make_async_remote_copy(
            there if source is None else source, there, ss, rs.at[n], device_id=device, device_id_type=MESH
        )
        copy.start()
        sends.append(rows)

    def arrived(name, block, row, rows):
        n = number(name)
        here = region(block, row, rows)
        pltpu.make_async_remote_copy(here, here, ss, rs.at[n], device_id=sib, device_id_type=MESH).wait_recv()

    mine = panel(0, 0)

    def turn(hh, src):
        row = hh * HALF_ROWS
        pltpu.make_async_copy(
            src.at[pl.ds(pl.multiple_of(c * PIECE, 16), PIECE)], region(mine, row, PIECE), own_sem.at[hh]
        ).start()
        for r in (0, 1, 2, 3, 6, 7, 4, 5):
            t = chan_target(r)
            piece = src.at[pl.ds(pl.multiple_of(t * PIECE, 16), PIECE)]
            if r:
                send(("a", hh * PER_HALF + r // AT_ONCE), mine, row + r * PIECE, PIECE, {"chan": t, "panel": p}, piece)
            if hh * PER_HALF + r // AT_ONCE not in Z_FIRST:
                send(("b", hh * PER_HALF + r // AT_ONCE), mine, row + r * PIECE, PIECE, {"chan": t, "panel": panel(0, 1)}, piece)

    shared = []

    def share(place_of, row, rows):
        send("share", panel(*place_of), row, rows, sib)
        shared.append(rows)

    def pass_on(what, dh, q):
        row, hh = q * CHUNK, q // PER_HALF
        z_first = q in Z_FIRST
        if what in ("own", "partner"):
            block = panel(0, dh)
            skip = 0
            if what == "own" and q % PER_HALF == 0:
                skip = PIECE
                here = region(block, row, PIECE)
                pltpu.make_async_copy(here, here, own_sem.at[hh]).wait()
            arrived(("a" if what == "own" else "b", q), block, row + skip, CHUNK - skip)
            send(("up", dh, q), block, row, CHUNK, up)
            send(("down", dh, q), block, row, CHUNK, down)
            if z_first:
                send(("y", 0, q), block, row, CHUNK, over)
            share((0, dh), row, CHUNK)
        elif what in ("near_up", "near_down"):
            dz, way, half = (3, up, 0) if what == "near_up" else (1, down, HALF)
            block = panel(dz, dh)
            arrived((what[5:], dh, q), block, row, CHUNK)
            send(("far_" + what[5:], dh, q), block, row + half, HALF, way)
            if z_first:
                send(("y", dz, q), block, row, CHUNK, over)
            share((dz, dh), row, CHUNK)
        elif what in ("far_up", "far_down"):
            at = row + (0 if what == "far_up" else HALF)
            arrived((what, dh, q), panel(2, dh), at, HALF)
            if z_first:
                send(("y2", at), panel(2, dh), at, HALF, over)
            share((2, dh), at, HALF)
        elif what in ("over2a", "over2b"):
            at = row + (0 if what == "over2a" else HALF)
            arrived(("y2", at), panel(2, 1), at, HALF)
            share((2, 1), at, HALF)
        else:
            dz = int(what[4])
            arrived(("y", dz, q), panel(dz, 1), row, CHUNK)
            share((dz, 1), row, CHUNK)

    channelize(0, half0)
    pl.semaphore_wait(barrier, len(greet))
    turn(0, half0)
    first = tuple(e for e in EVENTS if e[0] == "own" and e[2] < PER_HALF)

    def pass_first():
        for event in first:
            pass_on(*event)

    channelize(1, half1, pass_first)
    turn(1, half1)
    for event in EVENTS:
        if event in first:
            continue
        pass_on(*event)
    arrived("share", 0, 0, sum(shared))
    gone = out.at[pl.ds(0, sum(sends))]
    pltpu.make_async_remote_copy(gone, gone, ss, rs.at[0], device_id=sib, device_id_type=MESH).wait_send()


def spectra_of_all(volt, proto, gains, flagged, order):
    vm, sm = pl.BlockSpec(memory_space=pltpu.VMEM), pl.BlockSpec(memory_space=pltpu.SMEM)
    anywhere = pl.BlockSpec(memory_space=pl.ANY)
    return pl.pallas_call(
        spectra_kernel,
        out_shape=(
            jax.ShapeDtypeStruct((PANELS * BLOCK, 128), BF16),
            jax.ShapeDtypeStruct((8, 128), jnp.int32),
        ),
        in_specs=[anywhere, vm, vm, vm, sm, vm],
        out_specs=(anywhere, vm),
        scratch_shapes=[
            pltpu.VMEM((LOCAL, FALL * NFFT), BF16),
            pltpu.VMEM((TAPS * 128, NFFT), BF16),
            pltpu.VMEM((TAPS, FALL * HALF_IN, 128), F32),
            pltpu.VMEM((HALF_ROWS, 128), F32),
            pltpu.VMEM((HALF_ROWS, 128), BF16),
            pltpu.VMEM((HALF_ROWS, 128), BF16),
            pltpu.VMEM((128, 128), F32),
            pltpu.VMEM((GROUPS * 8, 128), F32),
            pltpu.VMEM((GROUPS * 8, 128), F32),
            pltpu.SemaphoreType.DMA((VOLT_COPIES,)),
            pltpu.SemaphoreType.DMA,
            pltpu.SemaphoreType.DMA((RECEIVES,)),
            pltpu.SemaphoreType.DMA((2,)),
        ],
        compiler_params=pltpu.CompilerParams(
            collective_id=0, has_side_effects=True, vmem_limit_bytes=56 * 2**20
        ),
        name="spectra",
    )(volt, proto, jnp.asarray(table_rows()), gains, flagged, order)


LOADS = 8
UNIT = 2 * 2 * PER


WIDTH = 256
COLUMNS = INPUTS // WIDTH


def correlate_kernel(place, spectra, out, raw, wide, sorted_, left, result, sems, out_sems):
    part = PANELS * BLOCK // LOADS

    def load(j):
        rows = pl.ds(j * part, part)
        return pltpu.make_async_copy(spectra.at[rows], raw.at[rows], sems.at[j])

    for j in range(LOADS):
        load(j).start()
    for j in range(LOADS):
        load(j).wait()

        def widen(i, _):
            rows = pl.ds(pl.multiple_of(j * part + i * 256, 256), 256)
            wide[rows, :] = raw[rows, :].astype(F32)
            return 0

        lax.fori_loop(0, part // 256, widen, 0)

    def sort(line, first, stations):
        for n in range(stations):
            row = pl.multiple_of(place[line, first + n], 8)
            sorted_[n * UNIT : (n + 1) * UNIT, :] = wide[pl.ds(row, UNIT), :]

    def part_of(e, rows):
        return sorted_[pl.ds(e, rows, stride=2 * PER), :].astype(BF16)

    p = lax.axis_index("panel")
    sort(p // 2, (p % 2) * 64, 64)
    for ch in range(PER):
        re, im = part_of(ch, 128), part_of(PER + ch, 128)
        left[ch, :128, :128] = re
        left[ch, :128, 128:] = im
        left[ch, 128:, :128] = im
        left[ch, 128:, 128:] = -re

    def write(b):
        columns = pl.ds(pl.multiple_of(b * WIDTH, WIDTH), WIDTH)
        return pltpu.make_async_copy(result.at[b], out.at[:, :, :, columns], out_sems.at[b])

    def block(b, _):
        sort(b, 0, WIDTH // 2)
        for ch in range(PER):
            right = jnp.concatenate([part_of(ch, WIDTH), part_of(PER + ch, WIDTH)], axis=1)
            prod = lax.dot_general(left[ch], right, NT, preferred_element_type=F32) * (1.0 / FRAMES)
            result[b, 0, ch] = prod[:128].astype(BF16)
            result[b, 1, ch] = prod[128:].astype(BF16)
        write(b).start()
        return 0

    lax.fori_loop(0, COLUMNS, block, 0)
    for b in range(COLUMNS):
        write(b).wait()


def correlate(place, spectra):
    return pl.pallas_call(
        correlate_kernel,
        out_shape=jax.ShapeDtypeStruct((2, PER, 128, INPUTS), BF16),
        in_specs=[pl.BlockSpec(memory_space=pltpu.SMEM), pl.BlockSpec(memory_space=pl.ANY)],
        out_specs=pl.BlockSpec(memory_space=pl.ANY),
        scratch_shapes=[
            pltpu.VMEM((PANELS * BLOCK, 128), BF16),
            pltpu.VMEM((PANELS * BLOCK, 128), F32),
            pltpu.VMEM((WIDTH // 2 * UNIT, 128), F32),
            pltpu.VMEM((PER, 256, 256), BF16),
            pltpu.VMEM((COLUMNS, 2, PER, 128, WIDTH), BF16),
            pltpu.SemaphoreType.DMA((LOADS,)),
            pltpu.SemaphoreType.DMA((COLUMNS,)),
        ],
        compiler_params=pltpu.CompilerParams(vmem_limit_bytes=56 * 2**20),
        cost_estimate=pl.CostEstimate(flops=2 * 6 * 256 * 2048 * 256, bytes_accessed=13 * 2**20, transcendentals=0),
        name="correlate",
    )(place, spectra)


def local(voltages, prototype, complex_gains, flagged, station_order):
    spectra, place = spectra_of_all(
        voltages, prototype, complex_gains, flagged, station_order.reshape(8, 128)
    )
    return correlate(place, spectra)


def solution(mesh):
    placed = (
        P(("chan", "panel"), None),
        P(),
        P(("chan", "panel"), None),
        P(("chan", "panel")),
        P(),
    )
    return jax.shard_map(
        local, mesh=mesh, in_specs=placed, out_specs=P(None, "chan", "panel", None), check_vma=False
    )
```

```python
import functools
import math

import jax
import jax.numpy as jnp
import numpy as np
from jax import lax
from jax.experimental import pallas as pl
from jax.experimental.pallas import tpu as pltpu
from jax.sharding import PartitionSpec as P

MESH = pl.DeviceIdType.MESH
F32, BF16 = jnp.float32, jnp.bfloat16
NT = (((1,), (1,)), ((), ()))

NFFT, TAPS, FRAMES, NCHAN = 4096, 4, 128, 48
INPUTS, STATIONS = 2048, 1024
LOCAL = 16
GROUPS, PER = 8, 6
FALL = FRAMES + TAPS - 1
HALF_IN = LOCAL // 2
PIECE = HALF_IN * 2 * PER
HALF_ROWS = GROUPS * PIECE
BLOCK = 2 * HALF_ROWS
PANELS = 16


def table_rows():
    n = np.arange(NFFT)[None, :]
    j = np.arange(NCHAN)[:, None]
    m = (n * (NFFT // 4 + j)) % NFFT
    phase = m.astype(np.float32) * np.float32(2.0 * math.pi / NFFT)
    both = np.stack([np.cos(phase), -np.sin(phase)], axis=1)
    both = both.reshape(GROUPS, PER, 2, NFFT).transpose(0, 2, 1, 3)
    both = np.pad(both, ((0, 0), (0, 0), (0, 8 - PER), (0, 0)))
    return both.reshape(128, NFFT).astype(jnp.bfloat16)


RECEIVES = 41
STEP_F = 34
STARTS = (0, 34, 66, 97)
VOLT_COPIES = 8

PER_HALF = 2
AT_ONCE = GROUPS // PER_HALF
CHUNK = HALF_ROWS // PER_HALF
HALF = CHUNK // 2
Z_FIRST = (0, 2)
EVENTS = (
    ("own", 0, 0),
    ("own", 0, 1),
    ("partner", 1, 1),
    ("near_up", 0, 0),
    ("near_down", 0, 0),
    ("over0", 1, 0),
    ("near_up", 0, 1),
    ("near_down", 0, 1),
    ("own", 0, 2),
    ("over3", 1, 0),
    ("near_up", 1, 1),
    ("near_down", 1, 1),
    ("own", 0, 3),
    ("partner", 1, 3),
    ("far_up", 0, 0),
    ("far_down", 0, 0),
    ("over1", 1, 0),
    ("far_up", 0, 1),
    ("far_down", 0, 1),
    ("over0", 1, 2),
    ("near_up", 0, 2),
    ("near_down", 0, 2),
    ("over2a", 1, 0),
    ("far_up", 1, 1),
    ("far_down", 1, 1),
    ("over2b", 1, 0),
    ("near_up", 0, 3),
    ("near_down", 0, 3),
    ("over3", 1, 2),
    ("near_up", 1, 3),
    ("near_down", 1, 3),
    ("over1", 1, 2),
    ("far_up", 0, 2),
    ("far_down", 0, 2),
    ("far_up", 0, 3),
    ("far_down", 0, 3),
    ("far_up", 1, 3),
    ("far_down", 1, 3),
    ("over2a", 1, 2),
    ("over2b", 1, 2),
)


def spectra_kernel(
    volt, proto, table, gains, flagged, order, out, place,
    buf, w, y, s, half0, half1, gt, gre, gim, vs, ss, rs, own_sem,
):
    c, p = lax.axis_index("chan"), lax.axis_index("panel")
    x, yl = c // 2, c % 2
    z, h, k = p // 4, (p // 2) % 2, p % 2

    def panel(dz, dh, dk=0):
        return ((z + dz) % 4) * 4 + ((h + dh) % 2) * 2 + (k + dk) % 2

    def at_panel(pan):
        return {"chan": c, "panel": pan}

    def chan_target(r):
        return ((x + 4 - r // 2) % 4) * 2 + (yl + r % 2) % 2

    up, down, over, sib = (at_panel(a) for a in (panel(1, 0), panel(3, 0), panel(0, 1), panel(0, 0, 1)))

    per = -(-FALL // VOLT_COPIES)
    cuts = [(a, min(per, FALL - a)) for a in range(0, FALL, per)]

    def load(i):
        cols = pl.ds(cuts[i][0] * NFFT, cuts[i][1] * NFFT)
        return pltpu.make_async_copy(volt.at[:, cols], buf.at[:, cols], vs.at[i])

    for i in range(len(cuts)):
        load(i).start()

    barrier = pltpu.get_barrier_semaphore()
    greet = [{"chan": chan_target(r), "panel": q} for r in range(1, GROUPS) for q in (p, panel(0, 1))]
    greet += [up, down, over, sib]
    for d in greet:
        pl.semaphore_signal(barrier, inc=1, device_id=d, device_id_type=MESH)

    tab = 512

    def weights(i, _):
        cols = pl.ds(pl.multiple_of(i * tab, tab), tab)
        t = table[:, cols].astype(F32)
        for tap in range(TAPS):
            w[pl.ds(tap * 128, 128), cols] = (t * proto[tap : tap + 1, cols]).astype(BF16)
        return 0

    lax.fori_loop(0, NFFT // tab, weights, 0)

    gt[...] = jnp.zeros_like(gt)
    gt[:LOCAL, : 2 * NCHAN] = gains[...]
    gt[...] = gt[...].T
    gre[...] = jnp.zeros_like(gre)
    gim[...] = jnp.zeros_like(gim)
    for g in range(GROUPS):
        gre[g * 8 : g * 8 + PER, :] = gt[pl.ds(g * 2 * PER, PER, stride=2), :]
        gim[g * 8 : g * 8 + PER, :] = gt[pl.ds(g * 2 * PER + 1, PER, stride=2), :]

    st = order[...]
    dev, within = st // HALF_IN, st % HALF_IN
    cs, ps = dev // PANELS, dev % PANELS
    r = ((cs // 2 - x + 4) % 4) * 2 + (cs % 2 + yl) % 2
    place[...] = ((ps * 2 + within // 4) * GROUPS + r) * PIECE + (within % 4) * (4 * PER)

    waited = [0]

    def channelize(hh, dest, between=None):
        low = hh * HALF_IN
        for first in STARTS:
            while waited[0] < len(cuts) and cuts[waited[0]][0] < first + STEP_F:
                load(waited[0]).wait()
                waited[0] += 1
            v = jnp.concatenate(
                [buf[low : low + HALF_IN, pl.ds((first + f) * NFFT, NFFT)] for f in range(STEP_F)], axis=0
            )
            rows = pl.ds(first * HALF_IN, STEP_F * HALF_IN)
            for j in range(2):
                prod = lax.dot_general(v, w[pl.ds(j * 256, 256), :], NT, preferred_element_type=F32)
                y[2 * j, rows, :] = prod[:, :128]
                y[2 * j + 1, rows, :] = prod[:, 128:]
        if between is not None:
            between()
        for i in range(HALF_IN):
            raw = y[0, pl.ds(i, FRAMES, stride=HALF_IN), :]
            for t in range(1, TAPS):
                raw = raw + y[t, pl.ds(t * HALF_IN + i, FRAMES, stride=HALF_IN), :]
            turned = raw.T
            n = low + i
            keep = (1 - flagged[n // 2]).astype(F32)
            for g in range(GROUPS):
                re, im = turned[g * 16 : g * 16 + 8], turned[g * 16 + 8 : g * 16 + 16]
                a, b = gre[g * 8 : g * 8 + 8, n : n + 1] * keep, gim[g * 8 : g * 8 + 8, n : n + 1] * keep
                at = g * PIECE + i * 2 * PER
                s[at : at + PER, :] = (a * re - b * im)[:PER]
                s[at + PER : at + 2 * PER, :] = (a * im + b * re)[:PER]
        dest[...] = s[...].astype(BF16)

    ids, sends = {}, []

    def number(name):
        return ids.setdefault(name, len(ids))

    def region(block, row, rows):
        return out.at[pl.ds(pl.multiple_of(block * BLOCK + row, 16), rows)]

    def send(name, block, row, rows, device, source=None):
        n = number(name)
        there = region(block, row, rows)
        copy = pltpu.make_async_remote_copy(
            there if source is None else source, there, ss, rs.at[n], device_id=device, device_id_type=MESH
        )
        copy.start()
        sends.append(rows)

    def arrived(name, block, row, rows):
        n = number(name)
        here = region(block, row, rows)
        pltpu.make_async_remote_copy(here, here, ss, rs.at[n], device_id=sib, device_id_type=MESH).wait_recv()

    mine = panel(0, 0)

    def turn(hh, src):
        row = hh * HALF_ROWS
        pltpu.make_async_copy(
            src.at[pl.ds(pl.multiple_of(c * PIECE, 16), PIECE)], region(mine, row, PIECE), own_sem.at[hh]
        ).start()
        for r in (0, 1, 2, 3, 6, 7, 4, 5):
            t = chan_target(r)
            piece = src.at[pl.ds(pl.multiple_of(t * PIECE, 16), PIECE)]
            if r:
                send(("a", hh * PER_HALF + r // AT_ONCE), mine, row + r * PIECE, PIECE, {"chan": t, "panel": p}, piece)
            if hh * PER_HALF + r // AT_ONCE not in Z_FIRST:
                send(("b", hh * PER_HALF + r // AT_ONCE), mine, row + r * PIECE, PIECE, {"chan": t, "panel": panel(0, 1)}, piece)

    shared = []

    def share(place_of, row, rows):
        send("share", panel(*place_of), row, rows, sib)
        shared.append(rows)

    def pass_on(what, dh, q):
        row, hh = q * CHUNK, q // PER_HALF
        z_first = q in Z_FIRST
        if what in ("own", "partner"):
            block = panel(0, dh)
            skip = 0
            if what == "own" and q % PER_HALF == 0:
                skip = PIECE
                here = region(block, row, PIECE)
                pltpu.make_async_copy(here, here, own_sem.at[hh]).wait()
            arrived(("a" if what == "own" else "b", q), block, row + skip, CHUNK - skip)
            send(("up", dh, q), block, row, CHUNK, up)
            send(("down", dh, q), block, row, CHUNK, down)
            if z_first:
                send(("y", 0, q), block, row, CHUNK, over)
            share((0, dh), row, CHUNK)
        elif what in ("near_up", "near_down"):
            dz, way, half = (3, up, 0) if what == "near_up" else (1, down, HALF)
            block = panel(dz, dh)
            arrived((what[5:], dh, q), block, row, CHUNK)
            send(("far_" + what[5:], dh, q), block, row + half, HALF, way)
            if z_first:
                send(("y", dz, q), block, row, CHUNK, over)
            share((dz, dh), row, CHUNK)
        elif what in ("far_up", "far_down"):
            at = row + (0 if what == "far_up" else HALF)
            arrived((what, dh, q), panel(2, dh), at, HALF)
            if z_first:
                send(("y2", at), panel(2, dh), at, HALF, over)
            share((2, dh), at, HALF)
        elif what in ("over2a", "over2b"):
            at = row + (0 if what == "over2a" else HALF)
            arrived(("y2", at), panel(2, 1), at, HALF)
            share((2, 1), at, HALF)
        else:
            dz = int(what[4])
            arrived(("y", dz, q), panel(dz, 1), row, CHUNK)
            share((dz, 1), row, CHUNK)

    channelize(0, half0)
    pl.semaphore_wait(barrier, len(greet))
    turn(0, half0)
    first = tuple(e for e in EVENTS if e[0] == "own" and e[2] < PER_HALF)

    def pass_first():
        for event in first:
            pass_on(*event)

    channelize(1, half1, pass_first)
    turn(1, half1)
    for event in EVENTS:
        if event in first:
            continue
        pass_on(*event)
    arrived("share", 0, 0, sum(shared))
    gone = out.at[pl.ds(0, sum(sends))]
    pltpu.make_async_remote_copy(gone, gone, ss, rs.at[0], device_id=sib, device_id_type=MESH).wait_send()


def spectra_of_all(volt, proto, gains, flagged, order):
    vm, sm = pl.BlockSpec(memory_space=pltpu.VMEM), pl.BlockSpec(memory_space=pltpu.SMEM)
    anywhere = pl.BlockSpec(memory_space=pl.ANY)
    return pl.pallas_call(
        spectra_kernel,
        out_shape=(
            jax.ShapeDtypeStruct((PANELS * BLOCK, 128), BF16),
            jax.ShapeDtypeStruct((8, 128), jnp.int32),
        ),
        in_specs=[anywhere, vm, vm, vm, sm, vm],
        out_specs=(anywhere, vm),
        scratch_shapes=[
            pltpu.VMEM((LOCAL, FALL * NFFT), BF16),
            pltpu.VMEM((TAPS * 128, NFFT), BF16),
            pltpu.VMEM((TAPS, FALL * HALF_IN, 128), F32),
            pltpu.VMEM((HALF_ROWS, 128), F32),
            pltpu.VMEM((HALF_ROWS, 128), BF16),
            pltpu.VMEM((HALF_ROWS, 128), BF16),
            pltpu.VMEM((128, 128), F32),
            pltpu.VMEM((GROUPS * 8, 128), F32),
            pltpu.VMEM((GROUPS * 8, 128), F32),
            pltpu.SemaphoreType.DMA((VOLT_COPIES,)),
            pltpu.SemaphoreType.DMA,
            pltpu.SemaphoreType.DMA((RECEIVES,)),
            pltpu.SemaphoreType.DMA((2,)),
        ],
        compiler_params=pltpu.CompilerParams(
            collective_id=0, has_side_effects=True, vmem_limit_bytes=56 * 2**20
        ),
        name="spectra",
    )(volt, proto, jnp.asarray(table_rows()), gains, flagged, order)


LOADS = 8
UNIT = 2 * 2 * PER


WIDTH = 256
COLUMNS = INPUTS // WIDTH


def correlate_kernel(place, spectra, out, raw, wide, sorted_, left, result, sems, out_sems):
    part = PANELS * BLOCK // LOADS

    def load(j):
        rows = pl.ds(j * part, part)
        return pltpu.make_async_copy(spectra.at[rows], raw.at[rows], sems.at[j])

    for j in range(LOADS):
        load(j).start()
    for j in range(LOADS):
        load(j).wait()

        def widen(i, _):
            rows = pl.ds(pl.multiple_of(j * part + i * 256, 256), 256)
            wide[rows, :] = raw[rows, :].astype(F32)
            return 0

        lax.fori_loop(0, part // 256, widen, 0)

    def sort(line, first, stations, slot):
        for n in range(stations):
            row = pl.multiple_of(place[line, first + n], 8)
            sorted_[slot, n * UNIT : (n + 1) * UNIT, :] = wide[pl.ds(row, UNIT), :]

    def part_of(e, rows, slot):
        return sorted_[slot, pl.ds(e, rows, stride=2 * PER), :].astype(BF16)

    p = lax.axis_index("panel")
    sort(p // 2, (p % 2) * 64, 64, 0)
    for ch in range(PER):
        re, im = part_of(ch, 128, 0), part_of(PER + ch, 128, 0)
        left[ch, :128, :128] = re
        left[ch, :128, 128:] = im
        left[ch, 128:, :128] = im
        left[ch, 128:, 128:] = -re

    def write(b):
        columns = pl.ds(pl.multiple_of(b * WIDTH, WIDTH), WIDTH)
        return pltpu.make_async_copy(result.at[b], out.at[:, :, :, columns], out_sems.at[b])

    def multiply(b, slot):
        for ch in range(PER):
            right = jnp.concatenate([part_of(ch, WIDTH, slot), part_of(PER + ch, WIDTH, slot)], axis=1)
            prod = lax.dot_general(left[ch], right, NT, preferred_element_type=F32) * (1.0 / FRAMES)
            result[b, 0, ch] = prod[:128].astype(BF16)
            result[b, 1, ch] = prod[128:].astype(BF16)
        write(b).start()

    def blocks(pair, _):
        b = 2 * pair
        sort(b + 1, 0, WIDTH // 2, 1)
        multiply(b, 0)
        sort(jnp.minimum(b + 2, COLUMNS - 1), 0, WIDTH // 2, 0)
        multiply(b + 1, 1)
        return 0

    sort(0, 0, WIDTH // 2, 0)
    lax.fori_loop(0, COLUMNS // 2, blocks, 0)
    for b in range(COLUMNS):
        write(b).wait()


def correlate(place, spectra):
    return pl.pallas_call(
        correlate_kernel,
        out_shape=jax.ShapeDtypeStruct((2, PER, 128, INPUTS), BF16),
        in_specs=[pl.BlockSpec(memory_space=pltpu.SMEM), pl.BlockSpec(memory_space=pl.ANY)],
        out_specs=pl.BlockSpec(memory_space=pl.ANY),
        scratch_shapes=[
            pltpu.VMEM((PANELS * BLOCK, 128), BF16),
            pltpu.VMEM((PANELS * BLOCK, 128), F32),
            pltpu.VMEM((2, WIDTH // 2 * UNIT, 128), F32),
            pltpu.VMEM((PER, 256, 256), BF16),
            pltpu.VMEM((COLUMNS, 2, PER, 128, WIDTH), BF16),
            pltpu.SemaphoreType.DMA((LOADS,)),
            pltpu.SemaphoreType.DMA((COLUMNS,)),
        ],
        compiler_params=pltpu.CompilerParams(vmem_limit_bytes=56 * 2**20),
        cost_estimate=pl.CostEstimate(flops=2 * 6 * 256 * 2048 * 256, bytes_accessed=13 * 2**20, transcendentals=0),
        name="correlate",
    )(place, spectra)


def local(voltages, prototype, complex_gains, flagged, station_order):
    spectra, place = spectra_of_all(
        voltages, prototype, complex_gains, flagged, station_order.reshape(8, 128)
    )
    return correlate(place, spectra)


def solution(mesh):
    placed = (
        P(("chan", "panel"), None),
        P(),
        P(("chan", "panel"), None),
        P(("chan", "panel")),
        P(),
    )
    return jax.shard_map(
        local, mesh=mesh, in_specs=placed, out_specs=P(None, "chan", "panel", None), check_vma=False
    )
```
